32 devices in a mesh: dp: 2 (over y), gx: 8 (over z, x), gy: 2 (over core).
Axes of the slice: x: 2, y: 2, z: 4, core: 2. Of those that a mesh axis runs over, the one named last changes fastest.
Arguments:
- fields: bfloat16 [2, 16, 256, 32768], P('dp', None, 'gx', 'gy'), may hold values from -6 to 6
- pre_act: bfloat16 [2, 16, 256, 32768], P('dp', None, 'gx', 'gy'), may hold values from -6 to 6
- cotangent: bfloat16 [2, 16, 256, 32768], P('dp', None, 'gx', 'gy'), may hold values from -6 to 6
- spec_weight: bfloat16 [2, 32, 32, 16, 256], P(None, 'gx', None, 'gy'), may hold values from -12 to 12
- point_weight: bfloat16 [16, 16], replicated, may hold values from -1.5 to 1.5
Outputs:
- grad_fields: bfloat16 [2, 16, 256, 32768], P('dp', None, 'gx', 'gy')
- grad_spec: float32 [2, 32, 32, 16, 256], P(None, 'gx', None, 'gy')
The draws below stay inside these ranges and needn't reach their ends.
All inputs are finite; a program needn't handle non-finite values.
Results may differ from the reference program's by a relative error of at most 0.0098.
Values may be sent and summed in bfloat16 or wider, within the bound.
A program may use at most 320 MiB of HBM per device.

```python
import math
import jax
import jax.numpy as jnp
from jax import lax

B = 2
C = 16
NX = 256
NY = 512
NZ = 64
MX = 32
MY = 32
MZ = 16
NYZ = 32768


def steps_of(own_key, extent, split, smallest, largest):
    def one(dim, parts):
        steps = jax.random.uniform(jax.random.fold_in(jax.random.fold_in(own_key, 6), dim), (parts,), jnp.float32, smallest / len(split), largest / len(split))
        return jnp.repeat(jnp.exp(steps), extent[dim] // parts).reshape((-1,) + (1,) * (len(extent) - dim - 1))

    loudness = one(*split[0])
    for cut in split[1:]:
        loudness = loudness * one(*cut)
    return loudness


def noise(own_key, dims, width, bound, pieces=(), kind=jnp.bfloat16):
    loudness = steps_of(own_key, dims, pieces, -0.22, 0.18) if pieces else 1.0
    drawn = jax.random.normal(own_key, dims, jnp.float32) * width * loudness
    return jnp.minimum(jnp.maximum(drawn, -bound), bound).astype(kind)


def setup_inputs(seed: int = 0) -> dict:
    key_of = jax.random.split(jax.random.key(seed), 6)
    fields = noise(key_of[0], (B, C, NX, NYZ), 1.0, 6.0, ((0, 2), (2, 8), (3, 2)))
    pre_act = noise(key_of[1], (B, C, NX, NYZ), 1.5, 6.0, ((0, 2), (2, 8), (3, 2)))
    cotangent = noise(key_of[2], (B, C, NX, NYZ), 1.0, 6.0, ((0, 2), (2, 8), (3, 2)))
    spec_weight = noise(key_of[3], (2, MX, MY, MZ, C * C), 3.0, 12.0, ((1, 8), (3, 2)))
    point_weight = noise(key_of[4], (C, C), C ** -0.5, 1.5)
    return {"fields": fields, "pre_act": pre_act, "cotangent": cotangent, "spec_weight": spec_weight, "point_weight": point_weight}


def kept_freqs(kept, length, both_signs):
    index = jnp.arange(kept, dtype=jnp.int32)
    if both_signs:
        return jnp.where(index < kept // 2, index, length - kept + index).astype(jnp.int32)
    return index

def phase(freqs, points, length):
    turns = points[:, None] * freqs[None, :] % length
    return turns.astype(jnp.float32) * (2.0 * math.pi / length)

def forward_table(kept, length):
    angle = phase(kept_freqs(kept, length, True), jnp.arange(length, dtype=jnp.int32), length)
    cosine = jnp.cos(angle)
    minus_sine = -jnp.sin(angle)
    upper = jnp.stack([cosine, minus_sine], axis=-1)
    lower = jnp.stack([-minus_sine, cosine], axis=-1)
    return jnp.stack([upper, lower], axis=1).astype(jnp.bfloat16)

def inverse_table(kept, length, positions):
    angle = phase(kept_freqs(kept, length, True), positions, length)
    cosine = jnp.transpose(jnp.cos(angle))
    sine = jnp.transpose(jnp.sin(angle))
    upper = jnp.stack([cosine, sine], axis=-1)
    lower = jnp.stack([-sine, cosine], axis=-1)
    return jnp.stack([upper, lower], axis=1).astype(jnp.bfloat16)

def z_forward_table():
    angle = phase(kept_freqs(MZ, NZ, False), jnp.arange(NZ, dtype=jnp.int32), NZ)
    return jnp.stack([jnp.cos(angle), -jnp.sin(angle)], axis=-1).reshape(NZ, 2 * MZ).astype(jnp.bfloat16)

def z_inverse_table():
    angle = jnp.transpose(phase(kept_freqs(MZ, NZ, False), jnp.arange(NZ, dtype=jnp.int32), NZ))
    return jnp.stack([jnp.cos(angle), -jnp.sin(angle)], axis=1).reshape(2 * MZ, NZ).astype(jnp.bfloat16)

def widen(table):
    return lax.optimization_barrier(table).astype(jnp.float32)

def gelu_slope(value):
    cdf = 0.5 * (1.0 + jax.scipy.special.erf(value * (1.0 / math.sqrt(2.0))))
    return cdf + value * jnp.exp(-0.5 * value * value) * (1.0 / math.sqrt(2.0 * math.pi))

def reference(fields, pre_act, cotangent, spec_weight, point_weight):
    highest = lax.Precision.HIGHEST
    grad_pre = (cotangent.astype(jnp.float32) * gelu_slope(pre_act.astype(jnp.float32))).astype(jnp.bfloat16)
    z_fwd = z_forward_table()
    x_fwd = widen(forward_table(MX, NX))
    y_fwd = widen(forward_table(MY, NY))
    y_back = widen(inverse_table(MY, NY, jnp.arange(NY, dtype=jnp.int32)))
    x_back = widen(inverse_table(MX, NX, jnp.arange(NX, dtype=jnp.int32)))
    z_back = z_inverse_table()
    stacked = jnp.concatenate([fields, grad_pre], axis=1).reshape(B * 2 * C, NX, NY, NZ)

    def forward_one(channel):
        z_spectra = jnp.dot(channel, z_fwd, preferred_element_type=jnp.float32).astype(jnp.bfloat16)
        z_spectra = z_spectra.reshape(NX, NY, MZ, 2).astype(jnp.float32)
        x_spectra = jnp.einsum('xyzr,xrkq->kyzq', z_spectra, x_fwd).astype(jnp.bfloat16)
        return jnp.einsum('kyzr,yrlq->klzq', x_spectra.astype(jnp.float32), y_fwd).astype(jnp.bfloat16)
    spectrum = lax.map(forward_one, stacked).reshape(B, 2, C, MX, MY, MZ, 2)
    field_hat = spectrum[:, 0].astype(jnp.float32)
    grad_hat_in = spectrum[:, 1].astype(jnp.float32)
    kz_index = jnp.arange(MZ, dtype=jnp.int32)
    weight_z = jnp.where(kz_index == 0, 1.0, 2.0).astype(jnp.float32) / float(NX * NY * NZ)
    scaled = grad_hat_in * weight_z[:, None]
    real_u, imag_u = (field_hat[..., 0], field_hat[..., 1])
    real_d, imag_d = (scaled[..., 0], scaled[..., 1])
    form = 'bixyz,boxyz->xyzio'
    real_w = jnp.einsum(form, real_u, real_d, precision=highest) + jnp.einsum(form, imag_u, imag_d, precision=highest)
    imag_w = jnp.einsum(form, real_u, imag_d, precision=highest) - jnp.einsum(form, imag_u, real_d, precision=highest)
    grad_spec = jnp.stack([real_w, imag_w], axis=0).reshape(2, MX, MY, MZ, C * C)
    weights = spec_weight.astype(jnp.float32).reshape(2, MX, MY, MZ, C, C)
    back_form = 'xyzio,boxyz->bixyz'
    real_g = jnp.einsum(back_form, weights[0], real_d, precision=highest) + jnp.einsum(back_form, weights[1], imag_d, precision=highest)
    imag_g = jnp.einsum(back_form, weights[0], imag_d, precision=highest) - jnp.einsum(back_form, weights[1], real_d, precision=highest)
    grad_hat = jnp.stack([real_g, imag_g], axis=-1).astype(jnp.bfloat16).reshape(B * C, MX, MY, MZ, 2)

    def inverse_one(channel):
        back_y = jnp.einsum('klzr,lryq->kyzq', channel.astype(jnp.float32), y_back).astype(jnp.bfloat16)
        back_x = jnp.einsum('kyzr,krxq->xyzq', back_y.astype(jnp.float32), x_back).astype(jnp.bfloat16)
        spectral = jnp.dot(back_x.reshape(NX, NY, 2 * MZ), z_back, preferred_element_type=jnp.float32)
        return spectral.reshape(NX, NY * NZ)
    spectral_part = lax.map(inverse_one, grad_hat).reshape(B, C, NX, NY * NZ)
    point_f = point_weight.astype(jnp.float32)
    outputs = []
    for sample in range(B):
        pointwise = jnp.einsum('io,oxq->ixq', point_f, grad_pre[sample].astype(jnp.float32))
        outputs.append((spectral_part[sample] + pointwise).astype(jnp.bfloat16))
    grad_fields = jnp.stack(outputs, axis=0)
    return (grad_fields, grad_spec)
```

```python
import functools
import math

import jax
import jax.numpy as jnp
import ml_dtypes
import numpy as np
from jax import lax
from jax.experimental import pallas as pl
from jax.experimental.pallas import tpu as pltpu
from jax.sharding import PartitionSpec as P

NZ = 64
ZGROUP = 4
VMEM_LIMIT = 56 * 1024 * 1024
BF16 = jnp.bfloat16
F32 = jnp.float32


def angles(kept, length, both_signs):
    freqs = np.arange(kept)
    if both_signs:
        freqs = np.where(freqs < kept // 2, freqs, length - kept + freqs)
    turns = np.arange(length)[:, None] * freqs[None, :] % length
    return (turns.astype(np.float32) * np.float32(2.0 * math.pi / length)).astype(np.float64)


def rounded(table):
    return np.asarray(table, np.float32).astype(ml_dtypes.bfloat16)


def forward_table(kept, length):
    angle = angles(kept, length, True)
    cosine, sine = np.cos(angle), np.sin(angle)
    upper = np.stack([cosine, -sine], axis=-1)
    lower = np.stack([sine, cosine], axis=-1)
    return np.stack([upper, lower], axis=1)


def z_table(kept, length, group):
    angle = angles(kept, length, False)
    parts = np.stack([np.cos(angle), -np.sin(angle)], axis=-1)
    table = np.einsum("zkr,yw->kyrwz", parts, np.eye(group))
    return rounded(table.reshape(kept * group * 2, group * length))


def x_tables(kept, length, count, channels):
    table = forward_table(kept, length).reshape(count, length // count, 2, kept, 2)
    big = np.einsum("dxrkq,ce->drcxkqe", table, np.eye(channels))
    rows = 2 * channels * (length // count)
    return rounded(big.reshape(count, rows, kept * 2 * channels))


def y_tables(kept, length, count):
    table = forward_table(kept, length).reshape(count, length // count, 2, kept, 2)
    return rounded(table.transpose(0, 4, 3, 1, 2).reshape(count, 2 * kept, -1))


def gelu_slope(value):
    size = jnp.abs(value)
    t = 1.0 / (1.0 + (0.3275911 / math.sqrt(2.0)) * size)
    decay = jnp.exp(value * value * -0.5)
    half_poly = t * (
        0.5 * 0.254829592
        + t
        * (
            0.5 * -0.284496736
            + t * (0.5 * 1.421413741 + t * (0.5 * -1.453152027 + t * (0.5 * 1.061405429)))
        )
    )
    lower = decay * (half_poly - size * (1.0 / math.sqrt(2.0 * math.pi)))
    return jnp.where(value < 0.0, lower, 1.0 - lower)


def dot(a, b, ca=1, cb=0):
    return lax.dot_general(a, b, (((ca,), (cb,)), ((), ())), preferred_element_type=F32)


def forward_kernel(dims, f_ref, p_ref, c_ref, zt_ref, yt_ref, xt_ref, gp_ref, out_ref, zs, ys):
    rows, block, kz_count, ky_count, row_block = dims
    chunk = pl.program_id(0)
    width = 2 * ZGROUP * NZ
    half = ZGROUP * NZ
    row_parts = rows // row_block
    piece = 16

    def body(step, carry):
        sub = step // row_parts
        part = step % row_parts
        lane = pl.multiple_of(sub * width, width)
        top = pl.multiple_of(part * row_block, row_block)
        for i in range(row_block // piece):
            at = (pl.ds(pl.multiple_of(top + i * piece, piece), piece), pl.ds(lane, width))
            slope = gelu_slope(p_ref[at].astype(F32))
            gp_ref[at] = (c_ref[at].astype(F32) * slope).astype(BF16)
        at = (pl.ds(top, row_block), pl.ds(lane, width))
        data = jnp.concatenate([f_ref[at], gp_ref[at]], axis=0)
        zt = zt_ref[...]
        spectra = [
            dot(zt, data[:, h * half : (h + 1) * half], 1, 1).reshape(
                kz_count, 2 * ZGROUP, 2 * row_block
            )
            for h in range(2)
        ]
        both = jnp.concatenate(spectra, axis=1).astype(BF16)
        line = chunk * (block // NZ * 2) + sub * (4 * ZGROUP)
        line = pl.multiple_of(line, 4 * ZGROUP)
        for kind in range(2):
            column = pl.multiple_of(kind * rows + top, row_block)
            zs[:, pl.ds(line, 4 * ZGROUP), pl.ds(column, row_block)] = both[
                :, :, kind * row_block : (kind + 1) * row_block
            ]
        return carry

    lax.fori_loop(0, (block // width) * row_parts, body, 0)

    @pl.when(chunk == pl.num_programs(0) - 1)
    def _():
        yt = yt_ref[...]

        def along_y(kz, carry):
            lines = dot(yt, zs[kz]).astype(BF16)
            top = pl.multiple_of(kz * ky_count, ky_count)
            for kind in range(2):
                for part in range(2):
                    ys[kind, pl.ds(top, ky_count), part * rows : (part + 1) * rows] = lines[
                        part * ky_count : (part + 1) * ky_count, kind * rows : (kind + 1) * rows
                    ]
            return carry

        lax.fori_loop(0, kz_count, along_y, 0)
        count_x, count_y, _, lines, lanes = out_ref.shape
        step = max(lanes, 256) // lanes
        for kind in range(2):
            for first in range(0, count_x, step):
                modes = dot(ys[kind], xt_ref[:, first * lanes : (first + step) * lanes])
                modes = modes.astype(BF16)
                for j in range(step):
                    out_ref[first + j, :, kind] = modes[:, j * lanes : (j + 1) * lanes].reshape(
                        count_y, lines, lanes
                    )


def modes_kernel(s_ref, own_ref, w_ref, e_ref, f_ref, spec_ref, hat_ref):
    n = f_ref.shape[0]

    def spread(values):
        wide = dot(values, e_ref[...])
        return [wide[:, j * n : (j + 1) * n] for j in range(4)]

    real = imag = 0.0
    for sample in range(s_ref.shape[0]):
        ur, ui, dr, di = spread(s_ref[sample])
        real = real + (ur * dr + ui * di)
        imag = imag + (ur * di - ui * dr)
    spec_ref[0] = real
    spec_ref[1] = imag
    _, _, dr, di = spread(own_ref[...])
    wr, wi = w_ref[0].astype(F32), w_ref[1].astype(F32)

    def over_outputs(terms):
        high = terms.astype(BF16)
        low = (terms - high.astype(F32)).astype(BF16)
        return dot(high, f_ref[...]) + dot(low, f_ref[...])

    hat_ref[...] = jnp.concatenate(
        [over_outputs(wr * dr + wi * di), over_outputs(wr * di - wi * dr)], axis=1
    ).astype(BF16)


def inverse_kernel(dims, g_ref, xt_ref, yi_ref, zi_ref, pw_ref, gp_ref, out_ref, gs, bs, zs):
    rows, block, kz_count, ky_count = dims
    chunk = pl.program_id(0)
    width = 2 * ZGROUP * NZ

    @pl.when(chunk == 0)
    def _():
        count_x, count_y, lines, lanes = g_ref.shape
        for d in range(count_x):
            gs[:, d * lanes : (d + 1) * lanes] = g_ref[d].reshape(count_y * lines, lanes)
        wide = min(256, rows)
        for part in range(2):
            for first in range(0, rows, wide):
                top = part * rows + first
                cells = dot(gs[...], xt_ref[top : top + wide, :], 1, 1).astype(BF16)
                bs[:, part * ky_count : (part + 1) * ky_count, first : first + wide] = (
                    cells.reshape(kz_count, ky_count, wide)
                )

        def along_y(kz, carry):
            zs[kz] = dot(yi_ref[...], bs[kz]).astype(BF16)
            return carry

        lax.fori_loop(0, kz_count, along_y, 0)

    def body(sub, carry):
        lane = pl.multiple_of(sub * width, width)
        line = chunk * (block // NZ * 2) + sub * (4 * ZGROUP)
        line = pl.multiple_of(line, 4 * ZGROUP)
        modes = zs[:, pl.ds(line, 4 * ZGROUP), :].reshape(kz_count * 4 * ZGROUP, rows)
        spectral = dot(modes, zi_ref[...], 0, 0)
        pointwise = dot(pw_ref[...], gp_ref[:, pl.ds(lane, width)])
        out_ref[:, pl.ds(lane, width)] = (spectral + pointwise).astype(BF16)
        return carry

    lax.fori_loop(0, block // width, body, 0)


def whole_block(shape):
    return pl.BlockSpec(shape, lambda *_: (0,) * len(shape))


def params():
    return pltpu.CompilerParams(
        dimension_semantics=("arbitrary",), vmem_limit_bytes=VMEM_LIMIT
    )


def on_device(fields, pre_act, cotangent, spec_weight, point_weight):
    count_x = lax.axis_size("gx")
    count_y = lax.axis_size("gy")
    _, channels, local_x, local_yz = fields.shape
    _, local_mx, my, local_mz, pairs = spec_weight.shape
    mx, mz = local_mx * count_x, local_mz * count_y
    nx = local_x * count_x
    local_y = local_yz // NZ
    ny = local_y * count_y
    rows = channels * local_x
    row_block = min(128, rows)
    block = min(1024, local_yz)
    lanes = local_mx * 2 * channels
    lines = local_mz * my
    modes = local_mx * my * local_mz
    at_x, at_y = lax.axis_index("gx"), lax.axis_index("gy")
    x_table = lax.dynamic_index_in_dim(
        jnp.asarray(x_tables(mx, nx, count_x, channels)), at_x, 0, keepdims=False
    )
    y_all = y_tables(my, ny, count_y)
    y_table = lax.dynamic_index_in_dim(jnp.asarray(y_all), at_y, 0, keepdims=False)
    y_inverse = lax.dynamic_index_in_dim(
        jnp.asarray(np.ascontiguousarray(y_all.transpose(0, 2, 1))), at_y, 0, keepdims=False
    )
    z_forward = jnp.asarray(z_table(mz, NZ, ZGROUP))
    z_inverse = jnp.asarray(z_table(mz, NZ, 2 * ZGROUP))

    flat = [array.reshape(rows, local_yz) for array in (fields, pre_act, cotangent)]
    tile = pl.BlockSpec((rows, block), lambda i: (0, i))
    grad_pre, partial = pl.pallas_call(
        functools.partial(forward_kernel, (rows, block, mz, my, row_block)),
        grid=(local_yz // block,),
        in_specs=[tile, tile, tile]
        + [whole_block(t.shape) for t in (z_forward, y_table, x_table)],
        out_specs=[tile, whole_block((count_x, count_y, 2, lines, lanes))],
        out_shape=[
            jax.ShapeDtypeStruct((rows, local_yz), BF16),
            jax.ShapeDtypeStruct((count_x, count_y, 2, lines, lanes), BF16),
        ],
        scratch_shapes=[
            pltpu.VMEM((mz, 2 * local_y, 2 * rows), BF16),
            pltpu.VMEM((2, mz * my, 2 * rows), BF16),
        ],
        compiler_params=params(),
        name="forward",
    )(*flat, z_forward, y_table, x_table)

    got = lax.all_to_all(partial, "gy", split_axis=1, concat_axis=1, tiled=True)
    summed = jnp.sum(got.astype(F32), axis=1).astype(BF16)
    got = lax.all_to_all(summed, "gx", split_axis=0, concat_axis=0, tiled=True)
    spectrum = jnp.sum(got.astype(F32), axis=0).astype(BF16)
    spectrum = spectrum.reshape(2, local_mz, my, local_mx, 2, channels)
    kz_index = at_y * local_mz + jnp.arange(local_mz, dtype=jnp.int32)
    weight_z = jnp.where(kz_index == 0, 1.0, 2.0).astype(F32) / float(nx * ny * NZ)
    weight = jnp.stack([jnp.ones_like(weight_z), weight_z], axis=0)
    spectrum = (spectrum.astype(F32) * weight[:, :, None, None, None, None]).astype(BF16)
    own = spectrum.transpose(3, 2, 1, 0, 4, 5).reshape(modes, 4 * channels)
    both = lax.all_gather(own, "dp", axis=0, tiled=False)

    eye = np.eye(channels)
    ones = np.ones((1, channels))
    by_input = np.kron(eye, ones)
    by_output = np.kron(ones, eye)
    expand = np.zeros((4 * channels, 4 * pairs))
    for j, part in enumerate((by_input, by_input, by_output, by_output)):
        expand[j * channels : (j + 1) * channels, j * pairs : (j + 1) * pairs] = part
    expand = jnp.asarray(rounded(expand))
    collect = jnp.asarray(rounded(by_input.T))
    weights = spec_weight.reshape(2, modes, pairs)
    part = min(256, modes)
    samples = both.shape[0]
    grad_spec, hat = pl.pallas_call(
        modes_kernel,
        grid=(modes // part,),
        in_specs=[
            pl.BlockSpec((samples, part, 4 * channels), lambda i: (0, i, 0)),
            pl.BlockSpec((part, 4 * channels), lambda i: (i, 0)),
            pl.BlockSpec((2, part, pairs), lambda i: (0, i, 0)),
            whole_block(expand.shape),
            whole_block(collect.shape),
        ],
        out_specs=[
            pl.BlockSpec((2, part, pairs), lambda i: (0, i, 0)),
            pl.BlockSpec((part, 2 * channels), lambda i: (i, 0)),
        ],
        out_shape=[
            jax.ShapeDtypeStruct((2, modes, pairs), F32),
            jax.ShapeDtypeStruct((modes, 2 * channels), BF16),
        ],
        compiler_params=params(),
        name="modes",
    )(both, own, weights, expand, collect)
    hat = hat.reshape(local_mx, my, local_mz, 2 * channels).transpose(2, 1, 0, 3)
    gathered = lax.all_gather(hat.reshape(lines, lanes), ("gx", "gy"), axis=0, tiled=False)
    gathered = gathered.reshape(count_x, count_y, lines, lanes)

    mixing = jnp.kron(point_weight, jnp.eye(local_x, dtype=BF16))
    grad_fields = pl.pallas_call(
        functools.partial(inverse_kernel, (rows, block, mz, my)),
        grid=(local_yz // block,),
        in_specs=[
            whole_block(t.shape) for t in (gathered, x_table, y_inverse, z_inverse, mixing)
        ]
        + [tile],
        out_specs=tile,
        out_shape=jax.ShapeDtypeStruct((rows, local_yz), BF16),
        scratch_shapes=[
            pltpu.VMEM((mz * my, count_x * lanes), BF16),
            pltpu.VMEM((mz, 2 * my, rows), BF16),
            pltpu.VMEM((mz, 2 * local_y, rows), BF16),
        ],
        compiler_params=params(),
        name="inverse",
    )(gathered, x_table, y_inverse, z_inverse, mixing, grad_pre)
    return (grad_fields.reshape(fields.shape), grad_spec.reshape(spec_weight.shape))


def solution(mesh):
    placed = (
        P("dp", None, "gx", "gy"),
        P("dp", None, "gx", "gy"),
        P("dp", None, "gx", "gy"),
        P(None, "gx", None, "gy", None),
        P(),
    )
    return jax.shard_map(
        on_device,
        mesh=mesh,
        in_specs=placed,
        out_specs=(P("dp", None, "gx", "gy"), P(None, "gx", None, "gy", None)),
        check_vma=False,
    )
```
